32 devices in a mesh: views: 8 (over y, x, core), slab: 4 (over z).
Axes of the slice: x: 2, y: 2, z: 4, core: 2. Of those that a mesh axis runs over, the one named last changes fastest.
Arguments:
- view_blocks: bfloat16 [8, 64, 64, 4096], P('views', 'slab'), may hold values from -6 to 6
- shifts: int32 [3, 8], replicated, may hold values from -512 to 512
- taps: float32 [3, 8, 4], replicated, may hold values from 0.1 to 0.7
- ztaps: float32 [3, 8, 3], replicated, may hold values from 0.15 to 0.6
Outputs:
- merged: bfloat16 [8, 64, 8, 4096], P('views', 'slab')
The draws below stay inside these ranges and needn't reach their ends.
All inputs are finite; a program needn't handle non-finite values.
Results may differ from the reference program's by a relative error of at most 0.0058.
Values may be sent and summed in bfloat16 or wider, within the bound.
A program may use at most 128 MiB of HBM per device.

```python
import jax
import jax.numpy as jnp
from jax import lax

C = 4096
RD = 64
TAPS = 4
LEVELS = 3
NVIEW = 8
NZ = 64


def plant(values, own_key, low, high):
    spot = [jax.random.randint(jax.random.fold_in(own_key, axis), (), 0, length) for axis, length in enumerate(values.shape)]
    longest = values.shape.index(max(values.shape))
    neighbour = spot[:longest] + [(spot[longest] + 1) % values.shape[longest]] + spot[longest + 1:]
    return values.at[tuple(spot)].set(low).at[tuple(neighbour)].set(high)


def level_of(own_key, extent, pieces, smallest, top_value):
    gain, own = 1.0, jax.random.fold_in(own_key, 6)
    for axis_at, blocks in pieces:
        steps = jnp.exp(jax.random.uniform(jax.random.fold_in(own, axis_at), (blocks,), jnp.float32, smallest / len(pieces), top_value / len(pieces)))
        gain = gain * jnp.repeat(steps, extent[axis_at] // blocks).reshape([-1 if axis == axis_at else 1 for axis in range(len(extent))])
    return gain


def bell_draw(rng, dims, deviation, limit, shards=(), kind=jnp.bfloat16):
    factor_of = level_of(rng, dims, shards, -0.22, 0.18) if shards else 1.0
    entries = jax.random.normal(rng, dims, jnp.float32) * deviation * factor_of
    return jnp.minimum(jnp.maximum(entries, -limit), limit).astype(kind)


def setup_inputs(seed: int = 0) -> dict:
    splits = jax.random.split(jax.random.key(seed), 5)
    return {
        "view_blocks": bell_draw(splits[0], (NVIEW, NZ, RD, C), 1.0, 6.0, ((0, 8), (1, 4))),
        "shifts": plant(jax.random.randint(splits[1], (LEVELS, NVIEW), 0 - C // 8, C // 8 + 1), jax.random.fold_in(splits[1], 1), 0 - C // 8, (C // 8 + 1) - 1).astype(jnp.int32),
        "taps": jnp.clip(jax.random.uniform(splits[2], (LEVELS, NVIEW, TAPS), jnp.float32, 0.1, 0.7), 0.1, 0.7),
        "ztaps": jnp.clip(jax.random.uniform(splits[3], (LEVELS, NVIEW, 3), jnp.float32, 0.15, 0.6), 0.15, 0.6),
    }


def transform(padded, zweights, cweights, shift):
    zmix = zweights[0] * padded[:, :-2].astype(jnp.float32)
    zmix = zmix + zweights[1] * padded[:, 1:-1].astype(jnp.float32)
    zmix = zmix + zweights[2] * padded[:, 2:].astype(jnp.float32)
    width = zmix.shape[3]
    margin = width // 8 + 2
    wide = jnp.pad(zmix, ((0, 0), (0, 0), (0, 0), (margin, margin)))
    total = jnp.zeros(zmix.shape, jnp.float32)
    for tap_index in range(cweights.shape[0]):
        start = (margin + shift + tap_index - 1).astype(jnp.int32)
        total = total + cweights[tap_index] * lax.dynamic_slice_in_dim(wide, start, width, 3)
    return total.astype(jnp.bfloat16)


def reference(view_blocks, shifts, taps, ztaps):
    block = view_blocks
    for level in range(LEVELS):
        groups = jnp.arange(NVIEW, dtype=jnp.int32) >> level
        level_shift = shifts[level][groups]
        level_taps = taps[level][groups]
        level_z = ztaps[level][groups]

        def one_view(items):
            image, zweights, cweights, shift = items
            padded = jnp.pad(image, ((1, 1), (0, 0), (0, 0)))
            return transform(padded[None], zweights, cweights, shift)[0]

        interp = lax.map(one_view, (block, level_z, level_taps, level_shift))
        rows = interp.shape[2]
        low = 2 ** level
        high = NVIEW // (2 * low)
        shaped = interp.reshape(high, 2, low, NZ, 2, rows // 2, C).astype(jnp.float32)
        summed = (0.5 * (shaped[:, 0] + shaped[:, 1])).astype(jnp.bfloat16)
        block = jnp.moveaxis(summed, 3, 1).reshape(NVIEW, NZ, rows // 2, C)
    return block
```

```python
import functools

import jax
import jax.numpy as jnp
from jax import lax
from jax.experimental import pallas as pl
from jax.experimental.pallas import tpu as pltpu
from jax.sharding import PartitionSpec as P

LANES = 128
BLOCK = 256
WINDOW = 512
STRIP = 512
MESH = pl.DeviceIdType.MESH


def kernel(
    pairs,
    width,
    margin,
    tap_count,
    x_hbm,
    shifts,
    taps,
    ztaps,
    out,
    xin,
    h0,
    mixed0,
    mixed1,
    mixed2,
    band,
    x1,
    s0,
    r0,
    h1s,
    h1r,
    x2,
    s1,
    r1,
    h2s,
    h2r,
    k2,
    s2,
    r2,
    load_sem,
    s0_sem,
    r0_sem,
    s1_sem,
    r1_sem,
    s2_sem,
    r2_sem,
    hs_sem,
    hr_sem,
):
    view = lax.axis_index("views")
    slab = lax.axis_index("slab")
    last_slab = lax.axis_size("slab") - 1
    planes = 2 * pairs
    bit0 = view % 2
    bit1 = (view // 2) % 2
    bit2 = (view // 4) % 2
    core_peer = view + 1 - 2 * bit0
    peer1 = view + 2 - 4 * bit1
    peer2 = view + 4 - 8 * bit2
    first = bit1
    second = bit2
    below = jnp.maximum(slab - 1, 0)
    above = jnp.minimum(slab + 1, last_slab)
    has_below = slab > 0
    has_above = slab < last_slab

    loads = [
        pltpu.make_async_copy(
            x_hbm.at[pl.ds(2 * p, 2)], xin.at[pl.ds(2 * p, 2)], load_sem.at[p]
        )
        for p in range(pairs)
    ]
    order0 = [(t + 1) % pairs for t in range(pairs)]
    for p in [0] + order0[:-1]:
        loads[p].start()

    barrier = pltpu.get_barrier_semaphore()
    for peer in (core_peer, peer1, peer2):
        pl.semaphore_signal(barrier, inc=1, device_id=(peer, slab), device_id_type=MESH)

    @pl.when(has_below)
    def _():
        pl.semaphore_signal(barrier, inc=1, device_id=(view, below), device_id_type=MESH)

    @pl.when(has_above)
    def _():
        pl.semaphore_signal(barrier, inc=1, device_id=(view, above), device_id_type=MESH)

    pl.semaphore_wait(
        barrier, 3 + has_below.astype(jnp.int32) + has_above.astype(jnp.int32)
    )

    def halo(level, src_down, src_up, landing):
        down = pltpu.make_async_remote_copy(
            src_down, landing.at[1], hs_sem.at[level, 0], hr_sem.at[level, 1],
            device_id=(view, below), device_id_type=MESH,
        )
        up = pltpu.make_async_remote_copy(
            src_up, landing.at[0], hs_sem.at[level, 1], hr_sem.at[level, 0],
            device_id=(view, above), device_id_type=MESH,
        )
        return down, up

    def when_do(condition, action):
        @pl.when(condition)
        def _():
            action()

    halo0 = halo(0, x_hbm.at[0], x_hbm.at[planes - 1], h0)
    halo1 = halo(1, h1s.at[0], h1s.at[1], h1r)
    halo2 = halo(2, h2s.at[0], h2s.at[1], h2r)
    when_do(has_below, halo0[0].start)
    when_do(has_above, halo0[1].start)

    def zero_ends(landing):
        @pl.when(jnp.logical_not(has_below))
        def _():
            landing[0] = jnp.zeros(landing.shape[1:], landing.dtype)

        @pl.when(jnp.logical_not(has_above))
        def _():
            landing[1] = jnp.zeros(landing.shape[1:], landing.dtype)

    for landing in (h0, h1r, h2r):
        zero_ends(landing)

    edge_blocks = margin // LANES
    mixes = [mixed0, mixed1, mixed2]
    for mixed in mixes:
        empty = jnp.zeros((edge_blocks,) + mixed.shape[1:], mixed.dtype)
        mixed[0:edge_blocks] = empty
        mixed[mixed.shape[0] - edge_blocks :] = empty

    groups = [view, view // 2, view // 4]
    bases = []
    for level in range(3):
        start = shifts[level, groups[level]] + (margin - 1)
        base = lax.div(start, jnp.int32(LANES))
        offset = start - base * LANES
        bases.append(base)
        distance = (
            lax.broadcasted_iota(jnp.int32, (WINDOW, BLOCK), 0)
            - lax.broadcasted_iota(jnp.int32, (WINDOW, BLOCK), 1)
            - offset
        )
        values = jnp.zeros((WINDOW, BLOCK), jnp.float32)
        for k in range(tap_count):
            values = jnp.where(distance == k, 0.5 * taps[level, groups[level], k], values)
        coarse = values.astype(jnp.bfloat16)
        band[level, 0] = coarse
        band[level, 1] = (values - coarse.astype(jnp.float32)).astype(jnp.bfloat16)

    def weights(level):
        return [ztaps[level, groups[level], i] for i in range(3)]

    def strips(body):
        def step(i, carry):
            body(pl.multiple_of(i * STRIP, STRIP))
            return carry

        lax.fori_loop(0, width // STRIP, step, 0)

    def f32(value):
        return value.astype(jnp.float32)

    def put(level, row, col, lower, upper):
        value = jnp.concatenate([lower, upper], 0).astype(jnp.bfloat16)
        at = lax.div(col, LANES) + edge_blocks
        for i in range(STRIP // LANES):
            mixes[level][at + i, row : row + 16, :] = value[:, i * LANES : (i + 1) * LANES]

    def mix_first(p):
        w = weights(0)

        def body(col):
            cols = pl.ds(col, STRIP)
            for part in range(2):
                side = bit0 if part == 0 else 1 - bit0
                for i in range(2):
                    rows = pl.ds(pl.multiple_of(32 * side + 16 * i, 16), 16)
                    a = f32(h0[0, rows, cols] if p == 0 else xin[2 * p - 1, rows, cols])
                    b = f32(xin[2 * p, rows, cols])
                    c = f32(xin[2 * p + 1, rows, cols])
                    d = f32(h0[1, rows, cols] if p == pairs - 1 else xin[2 * p + 2, rows, cols])
                    lower = w[0] * a + w[1] * b + w[2] * c
                    upper = w[0] * b + w[1] * c + w[2] * d
                    put(0, 64 * part + 32 * i, col, lower[:8], upper[:8])
                    put(0, 64 * part + 32 * i + 16, col, lower[8:], upper[8:])

        strips(body)

    def mix_later(level, p, source, landing, chunk_starts):
        w = weights(level)

        def body(col):
            cols = pl.ds(col, STRIP)
            for at, chunk in enumerate(chunk_starts):
                even = at % 2 if len(chunk_starts) > 2 else None
                rows = pl.ds(pl.multiple_of(16 * chunk, 16), 16)
                here = f32(source[p, rows, cols])
                b, c = here[:8], here[8:]

                def edge(end):
                    if even is None:
                        block = f32(landing[end, 0:16, cols])
                        return jnp.where(chunk == 0, block[:8], block[8:])
                    block = f32(
                        landing[end, pl.ds(pl.multiple_of(8 * (chunk - even), 16), 16), cols]
                    )
                    return block[8 * even : 8 * even + 8]

                a = edge(0) if p == 0 else f32(source[p - 1, rows, cols])[8:]
                d = edge(1) if p == pairs - 1 else f32(source[p + 1, rows, cols])[:8]
                lower = w[0] * a + w[1] * b + w[2] * c
                upper = w[0] * b + w[1] * c + w[2] * d
                put(level, 16 * at, col, lower, upper)

        strips(body)

    def interpolate(level, p, rows, kept, sent):
        together = max(1, 512 // rows)
        base = bases[level]
        mixed = mixes[level]
        half = rows // 2

        def step(group, carry):
            windows = []
            for j in range(together):
                at = base + (BLOCK // LANES) * (group * together + j)
                windows.append(
                    jnp.concatenate([mixed[at + i] for i in range(WINDOW // LANES)], 1)
                )
            operand = jnp.concatenate(windows, 0)
            total = jnp.dot(operand, band[level, 0], preferred_element_type=jnp.float32)
            total += jnp.dot(operand, band[level, 1], preferred_element_type=jnp.float32)
            for j in range(together):
                cols = pl.ds(pl.multiple_of((group * together + j) * BLOCK, BLOCK), BLOCK)
                piece = total[j * rows : (j + 1) * rows].astype(jnp.bfloat16)
                kept[p, :, cols] = piece[:half]
                sent[p, :, cols] = piece[half:]
            return carry

        lax.fori_loop(0, width // (BLOCK * together), step, 0)

    def add_into(target, p, kept, received):
        def body(col):
            cols = pl.ds(col, STRIP)
            target[p, :, cols] = (f32(kept[p, :, cols]) + f32(received[p, :, cols])).astype(
                jnp.bfloat16
            )

        strips(body)

    def exchange(sent, received, send_sem, recv_sem, peer):
        return [
            pltpu.make_async_remote_copy(
                sent.at[p], received.at[p], send_sem.at[p], recv_sem.at[p],
                device_id=(peer, slab), device_id_type=MESH,
            )
            for p in range(pairs)
        ]

    cross0 = exchange(s0, r0, s0_sem, r0_sem, core_peer)
    cross1 = exchange(s1, r1, s1_sem, r1_sem, peer1)
    cross2 = exchange(s2, r2, s2_sem, r2_sem, peer2)

    def send_edges(p, source, ready, copies, chunks):
        for end, at, half in ((0, 0, 0), (1, pairs - 1, 8)):
            if p != at:
                continue

            def body(col):
                cols = pl.ds(col, STRIP)
                for c in range(0, chunks, 2):
                    one = f32(source[p, 16 * c : 16 * c + 16, cols])[half : half + 8]
                    two = f32(source[p, 16 * c + 16 : 16 * c + 32, cols])[half : half + 8]
                    ready[end, 8 * c : 8 * c + 16, cols] = jnp.concatenate([one, two], 0).astype(
                        jnp.bfloat16
                    )

            strips(body)
            when_do(has_below if end == 0 else has_above, copies[end].start)

    loaded = set()

    def need(p):
        if 0 <= p < pairs and p not in loaded:
            loads[p].wait()
            loaded.add(p)

    def await_halo(p, copies):
        if p == 0:
            when_do(has_below, copies[1].wait_recv)
        if p == pairs - 1:
            when_do(has_above, copies[0].wait_recv)

    def level0(p):
        for q in (p - 1, p, p + 1):
            need(q)
        await_halo(p, halo0)
        mix_first(p)
        interpolate(0, p, 128, x1, s0)
        cross0[p].start()

    def merge0(p):
        cross0[p].wait_recv()
        add_into(x1, p, x1, r0)
        send_edges(p, x1, h1s, halo1, 4)

    def level1(p):
        await_halo(p, halo1)
        own, other = 2 * first, 2 - 2 * first
        mix_later(1, p, x1, h1r, [own, own + 1, other, other + 1])
        interpolate(1, p, 64, x2, s1)
        cross1[p].start()

    def merge1(p):
        cross1[p].wait_recv()
        add_into(x2, p, x2, r1)
        send_edges(p, x2, h2s, halo2, 2)

    def level2(p):
        await_halo(p, halo2)
        mix_later(2, p, x2, h2r, [second, 1 - second])
        interpolate(2, p, 32, k2, s2)
        cross2[p].start()

    def merge2(p):
        cross2[p].wait_recv()
        add_into(out, p, k2, r2)

    for t in range(pairs + 3):
        if t < pairs:
            level0((t + 1) % pairs)
        if 1 <= t <= pairs:
            merge0(t % pairs)
        if t >= 3:
            level1((t - 1) % pairs)
    for t in range(pairs + 3):
        if t < pairs:
            merge1((t + 2) % pairs)
        if 2 <= t < pairs + 2:
            level2((t + 1) % pairs)
        if 3 <= t:
            merge2(t % pairs)

    for copies in (cross0, cross1, cross2):
        for copy in copies:
            copy.wait_send()
    for copies in (halo0, halo1, halo2):
        when_do(has_below, copies[0].wait_send)
        when_do(has_above, copies[1].wait_send)


def shards(view_blocks, shifts, taps, ztaps):
    _, planes, rows, width = view_blocks.shape
    pairs = planes // 2
    margin = width // 8 + LANES
    blocks = (width + 2 * margin) // LANES
    bf16 = jnp.bfloat16
    dma = pltpu.SemaphoreType.DMA
    vmem = pltpu.VMEM
    result = pl.pallas_call(
        functools.partial(kernel, pairs, width, margin, taps.shape[2]),
        out_shape=jax.ShapeDtypeStruct((pairs, 16, width), bf16),
        in_specs=[pl.BlockSpec(memory_space=pl.ANY)]
        + [pl.BlockSpec(memory_space=pltpu.SMEM)] * 3,
        out_specs=pl.BlockSpec(memory_space=pltpu.VMEM),
        scratch_shapes=[
            vmem((planes, rows, width), bf16),
            vmem((2, rows, width), bf16),
            vmem((blocks, 2 * rows, LANES), bf16),
            vmem((blocks, rows, LANES), bf16),
            vmem((blocks, rows // 2, LANES), bf16),
            vmem((3, 2, WINDOW, BLOCK), bf16),
            vmem((pairs, rows, width), bf16),
            vmem((pairs, rows, width), bf16),
            vmem((pairs, rows, width), bf16),
            vmem((2, rows // 2, width), bf16),
            vmem((2, rows // 2, width), bf16),
            vmem((pairs, rows // 2, width), bf16),
            vmem((pairs, rows // 2, width), bf16),
            vmem((pairs, rows // 2, width), bf16),
            vmem((2, rows // 4, width), bf16),
            vmem((2, rows // 4, width), bf16),
            vmem((pairs, rows // 4, width), bf16),
            vmem((pairs, rows // 4, width), bf16),
            vmem((pairs, rows // 4, width), bf16),
            dma((pairs,)),
            dma((pairs,)),
            dma((pairs,)),
            dma((pairs,)),
            dma((pairs,)),
            dma((pairs,)),
            dma((pairs,)),
            dma((3, 2)),
            dma((3, 2)),
        ],
        compiler_params=pltpu.CompilerParams(
            collective_id=0, has_side_effects=True, vmem_limit_bytes=58 * 1024 * 1024
        ),
        cost_estimate=pl.CostEstimate(
            flops=15_000_000_000, bytes_accessed=9 * 1024 * 1024, transcendentals=0
        ),
    )(view_blocks.reshape(planes, rows, width), shifts, taps, ztaps)
    return result.reshape(1, planes, 8, width)


def solution(mesh):
    return jax.shard_map(
        shards,
        mesh=mesh,
        in_specs=(P("views", "slab", None, None), P(), P(), P()),
        out_specs=P("views", "slab", None, None),
        check_vma=False,
    )
```

```python
import functools

import jax
import jax.numpy as jnp
from jax import lax
from jax.experimental import pallas as pl
from jax.experimental.pallas import tpu as pltpu
from jax.sharding import PartitionSpec as P

LANES = 128
BLOCK = 256
WINDOW = 512
STRIP = 512
MESH = pl.DeviceIdType.MESH


def kernel(
    pairs,
    width,
    margin,
    tap_count,
    x_hbm,
    shifts,
    taps,
    ztaps,
    out,
    xin,
    h0,
    mixed0,
    mixed1,
    mixed2,
    band,
    x1,
    s0,
    r0,
    h1s,
    h1r,
    x2,
    s1,
    r1,
    h2s,
    h2r,
    y1,
    h3s,
    h3r,
    k2,
    s2,
    r2,
    load_sem,
    s0_sem,
    r0_sem,
    s1_sem,
    r1_sem,
    s2_sem,
    r2_sem,
    hs_sem,
    hr_sem,
):
    view = lax.axis_index("views")
    slab = lax.axis_index("slab")
    last_slab = lax.axis_size("slab") - 1
    planes = 2 * pairs
    bit0 = view % 2
    bit1 = (view // 2) % 2
    bit2 = (view // 4) % 2
    core_peer = view + 1 - 2 * bit0
    near = view + 2 - 4 * bit1
    far = view + 4 - 8 * bit2
    peer1 = near + bit0 * (far - near)
    peer2 = far + bit0 * (near - far)
    first = bit1 + bit0 * (bit2 - bit1)
    second = bit2 + bit0 * (bit1 - bit2)
    even_core = bit0 == 0
    odd_core = bit0 == 1
    below = jnp.maximum(slab - 1, 0)
    above = jnp.minimum(slab + 1, last_slab)
    has_below = slab > 0
    has_above = slab < last_slab

    loads = [
        pltpu.make_async_copy(
            x_hbm.at[pl.ds(2 * p, 2)], xin.at[pl.ds(2 * p, 2)], load_sem.at[p]
        )
        for p in range(pairs)
    ]
    order0 = [(t + 1) % pairs for t in range(pairs)]
    for p in [0] + order0[:-1]:
        loads[p].start()

    barrier = pltpu.get_barrier_semaphore()
    for peer in (core_peer, peer1, peer2):
        pl.semaphore_signal(barrier, inc=1, device_id=(peer, slab), device_id_type=MESH)

    @pl.when(has_below)
    def _():
        pl.semaphore_signal(barrier, inc=1, device_id=(view, below), device_id_type=MESH)

    @pl.when(has_above)
    def _():
        pl.semaphore_signal(barrier, inc=1, device_id=(view, above), device_id_type=MESH)

    pl.semaphore_wait(
        barrier, 3 + has_below.astype(jnp.int32) + has_above.astype(jnp.int32)
    )

    def halo(level, src_down, src_up, landing):
        down = pltpu.make_async_remote_copy(
            src_down, landing.at[1], hs_sem.at[level, 0], hr_sem.at[level, 1],
            device_id=(view, below), device_id_type=MESH,
        )
        up = pltpu.make_async_remote_copy(
            src_up, landing.at[0], hs_sem.at[level, 1], hr_sem.at[level, 0],
            device_id=(view, above), device_id_type=MESH,
        )
        return down, up

    def when_do(condition, action):
        @pl.when(condition)
        def _():
            action()

    halo0 = halo(0, x_hbm.at[0], x_hbm.at[planes - 1], h0)
    halo1 = halo(1, h1s.at[0], h1s.at[1], h1r)
    halo2 = halo(2, h2s.at[0], h2s.at[1], h2r)
    halo3 = halo(3, h3s.at[0], h3s.at[1], h3r)
    when_do(has_below, halo0[0].start)
    when_do(has_above, halo0[1].start)

    def zero_ends(landing):
        @pl.when(jnp.logical_not(has_below))
        def _():
            landing[0] = jnp.zeros(landing.shape[1:], landing.dtype)

        @pl.when(jnp.logical_not(has_above))
        def _():
            landing[1] = jnp.zeros(landing.shape[1:], landing.dtype)

    for landing in (h0, h1r, h2r, h3r):
        zero_ends(landing)

    edge_blocks = margin // LANES
    mixes = [mixed0, mixed1, mixed2]
    for mixed in mixes:
        empty = jnp.zeros((edge_blocks,) + mixed.shape[1:], mixed.dtype)
        mixed[0:edge_blocks] = empty
        mixed[mixed.shape[0] - edge_blocks :] = empty

    groups = [view, view // 2, view // 4]
    bases = []
    scales = []
    candidates = 1.0 + (
        lax.broadcasted_iota(jnp.int32, (8, LANES), 0) * LANES
        + lax.broadcasted_iota(jnp.int32, (8, LANES), 1)
    ).astype(jnp.float32) * (1.0 / (8 * LANES))
    for level in range(3):
        start = shifts[level, groups[level]] + (margin - 1)
        base = lax.div(start, jnp.int32(LANES))
        offset = start - base * LANES
        bases.append(base)
        distance = (
            lax.broadcasted_iota(jnp.int32, (WINDOW, BLOCK), 0)
            - lax.broadcasted_iota(jnp.int32, (WINDOW, BLOCK), 1)
            - offset
        )
        worst = jnp.zeros((8, LANES), jnp.float32)
        for k in range(tap_count):
            tap = taps[level, groups[level], k]
            exact = tap * candidates
            missed = jnp.abs(exact.astype(jnp.bfloat16).astype(jnp.float32) - exact)
            worst = jnp.maximum(worst, missed / jnp.maximum(exact, 1e-30))
        chosen = jnp.where(worst == jnp.min(worst), candidates, 0.0)
        scale = jnp.max(chosen)
        scales.append(1.0 / scale)
        values = jnp.zeros((WINDOW, BLOCK), jnp.float32)
        for k in range(tap_count):
            values = jnp.where(distance == k, taps[level, groups[level], k] * scale, values)
        band[level] = (0.5 * values).astype(jnp.bfloat16)

    def weights(level):
        return [ztaps[level, groups[level], i] * scales[level] for i in range(3)]

    def strips(body):
        def step(i, carry):
            body(pl.multiple_of(i * STRIP, STRIP))
            return carry

        lax.fori_loop(0, width // STRIP, step, 0)

    def f32(value):
        return value.astype(jnp.float32)

    def put(level, row, col, lower, upper):
        value = jnp.concatenate([lower, upper], 0).astype(jnp.bfloat16)
        at = lax.div(col, LANES) + edge_blocks
        for i in range(STRIP // LANES):
            mixes[level][at + i, pl.ds(row, 16), :] = value[:, i * LANES : (i + 1) * LANES]

    def mix_first(p):
        w = weights(0)

        def body(col):
            cols = pl.ds(col, STRIP)
            for part in range(2):
                side = bit0 if part == 0 else 1 - bit0
                for i in range(2):
                    rows = pl.ds(pl.multiple_of(32 * side + 16 * i, 16), 16)
                    a = f32(h0[0, rows, cols] if p == 0 else xin[2 * p - 1, rows, cols])
                    b = f32(xin[2 * p, rows, cols])
                    c = f32(xin[2 * p + 1, rows, cols])
                    d = f32(h0[1, rows, cols] if p == pairs - 1 else xin[2 * p + 2, rows, cols])
                    lower = w[0] * a + w[1] * b + w[2] * c
                    upper = w[0] * b + w[1] * c + w[2] * d
                    slots = (0, 1 + side) if i == 0 else (2 - side, 3)
                    for half in range(2):
                        row = pl.multiple_of(64 * part + 16 * slots[half], 16)
                        put(
                            0, row, col,
                            lower[8 * half : 8 * half + 8],
                            upper[8 * half : 8 * half + 8],
                        )

        strips(body)

    def mix_later(level, p, target, source, landing, chunk_starts):
        w = weights(level)

        def body(col):
            cols = pl.ds(col, STRIP)
            for at, chunk in enumerate(chunk_starts):
                even = at % 2 if len(chunk_starts) > 2 else None
                rows = pl.ds(pl.multiple_of(16 * chunk, 16), 16)
                here = f32(source[p, rows, cols])
                b, c = here[:8], here[8:]

                def edge(end):
                    if even is None:
                        block = f32(landing[end, 0:16, cols])
                        return jnp.where(chunk == 0, block[:8], block[8:])
                    block = f32(
                        landing[end, pl.ds(pl.multiple_of(8 * (chunk - even), 16), 16), cols]
                    )
                    return block[8 * even : 8 * even + 8]

                a = edge(0) if p == 0 else f32(source[p - 1, rows, cols])[8:]
                d = edge(1) if p == pairs - 1 else f32(source[p + 1, rows, cols])[:8]
                lower = w[0] * a + w[1] * b + w[2] * c
                upper = w[0] * b + w[1] * c + w[2] * d
                put(target, 16 * at, col, lower, upper)

        strips(body)

    def interpolate(level, p, target, kept, sent):
        mixed = mixes[target]
        rows = mixed.shape[1]
        together = max(1, 512 // rows)
        base = bases[level]
        half = rows // 2

        def step(group, carry):
            windows = []
            for j in range(together):
                at = base + (BLOCK // LANES) * (group * together + j)
                windows.append(
                    jnp.concatenate([mixed[at + i] for i in range(WINDOW // LANES)], 1)
                )
            operand = jnp.concatenate(windows, 0)
            total = jnp.dot(operand, band[level], preferred_element_type=jnp.float32)
            for j in range(together):
                cols = pl.ds(pl.multiple_of((group * together + j) * BLOCK, BLOCK), BLOCK)
                piece = total[j * rows : (j + 1) * rows].astype(jnp.bfloat16)
                kept[p, :, cols] = piece[:half]
                sent[p, :, cols] = piece[half:]
            return carry

        lax.fori_loop(0, width // (BLOCK * together), step, 0)

    def add_into(target, p, kept, received):
        def body(col):
            cols = pl.ds(col, STRIP)
            target[p, :, cols] = (f32(kept[p, :, cols]) + f32(received[p, :, cols])).astype(
                jnp.bfloat16
            )

        strips(body)

    def exchange(sent, received, send_sem, recv_sem, peer):
        return [
            pltpu.make_async_remote_copy(
                sent.at[p], received.at[p], send_sem.at[p], recv_sem.at[p],
                device_id=(peer, slab), device_id_type=MESH,
            )
            for p in range(pairs)
        ]

    cross0 = exchange(s0, r0, s0_sem, r0_sem, core_peer)
    cross1 = exchange(s1, r1, s1_sem, r1_sem, peer1)
    cross2 = exchange(s2, r2, s2_sem, r2_sem, peer2)
    sent_rows = pl.ds(pl.multiple_of(16 - 16 * second, 16), 16)
    kept_rows = pl.ds(pl.multiple_of(16 * second, 16), 16)
    cross3 = exchange(x2.at[:, sent_rows], r2, s2_sem, r2_sem, peer2)

    def send_edges(p, source, ready, copies, chunks):
        for end, at, half in ((0, 0, 0), (1, pairs - 1, 8)):
            if p != at:
                continue

            def body(col):
                cols = pl.ds(col, STRIP)
                for c in range(0, chunks, 2):
                    one = f32(source[p, 16 * c : 16 * c + 16, cols])[half : half + 8]
                    two = f32(source[p, 16 * c + 16 : 16 * c + 32, cols])[half : half + 8]
                    ready[end, 8 * c : 8 * c + 16, cols] = jnp.concatenate([one, two], 0).astype(
                        jnp.bfloat16
                    )

            strips(body)
            when_do(has_below if end == 0 else has_above, copies[end].start)

    loaded = set()

    def need(p):
        if 0 <= p < pairs and p not in loaded:
            loads[p].wait()
            loaded.add(p)

    def await_halo(p, copies):
        if p == 0:
            when_do(has_below, copies[1].wait_recv)
        if p == pairs - 1:
            when_do(has_above, copies[0].wait_recv)

    def level0(p):
        for q in (p - 1, p, p + 1):
            need(q)
        await_halo(p, halo0)
        mix_first(p)
        interpolate(0, p, 0, x1, s0)
        cross0[p].start()

    def merge0(p):
        cross0[p].wait_recv()
        add_into(x1, p, x1, r0)
        send_edges(p, x1, h1s, halo1, 4)

    own, other = 2 * first, 2 - 2 * first

    def level1_even(p):
        mix_later(1, p, 1, x1, h1r, [own, own + 1, other, other + 1])
        interpolate(1, p, 1, x2, s1)
        cross1[p].start()

    def merge1_even(p):
        cross1[p].wait_recv()
        add_into(x2, p, x2, r1)
        send_edges(p, x2, h2s, halo2, 2)

    def level2_even(p):
        await_halo(p, halo2)
        mix_later(2, p, 2, x2, h2r, [second, 1 - second])
        interpolate(2, p, 2, k2, s2)
        cross2[p].start()

    def merge2_even(p):
        cross2[p].wait_recv()
        add_into(out, p, k2, r2)

    def level1_odd(p):
        mix_later(1, p, 1, x1, h1r, [0, 1, 2, 3])
        interpolate(1, p, 1, y1.at[:, 0:32], y1.at[:, 32:64])
        send_edges(p, y1, h3s, halo3, 4)

    def level2_odd(p):
        await_halo(p, halo3)
        mix_later(2, p, 1, y1, h3r, [own, own + 1, other, other + 1])
        interpolate(2, p, 1, x2, s1)
        cross1[p].start()

    def merge1_odd(p):
        cross1[p].wait_recv()
        add_into(x2, p, x2, r1)
        cross3[p].start()

    def merge2_odd(p):
        cross3[p].wait_recv()
        add_into(out, p, x2.at[:, kept_rows], r2)

    odd_slots = [(t, (t - 2) % pairs) for t in range(5, pairs + 1)]
    odd_slots += [(t, (t - 3) % pairs) for t in range(pairs + 2, pairs + 6)]
    odd_order = dict(odd_slots)
    odd_list = [p for _, p in odd_slots]

    for t in range(pairs + 3):
        if t < pairs:
            level0((t + 1) % pairs)
        if 1 <= t <= pairs:
            merge0(t % pairs)
        if t >= 3:
            p = (t - 1) % pairs
            await_halo(p, halo1)

            @pl.when(even_core)
            def _():
                level1_even(p)

            @pl.when(odd_core)
            def _():
                level1_odd(p)
                if t in odd_order:
                    level2_odd(odd_order[t])
                    at = odd_list.index(odd_order[t])
                    if at >= 2:
                        merge1_odd(odd_list[at - 2])

    @pl.when(even_core)
    def _():
        for t in range(pairs + 3):
            if t < pairs:
                merge1_even((t + 2) % pairs)
            if 2 <= t < pairs + 2:
                level2_even((t + 1) % pairs)
            if 3 <= t:
                merge2_even(t % pairs)
        for p in range(pairs):
            cross2[p].wait_send()
        when_do(has_below, halo2[0].wait_send)
        when_do(has_above, halo2[1].wait_send)

    @pl.when(odd_core)
    def _():
        begun = sum(1 for t, _ in odd_slots if t < pairs + 3)
        for at in range(begun, pairs + 2):
            if at < pairs:
                level2_odd(odd_list[at])
            merge1_odd(odd_list[at - 2])
            if at - begun >= 1:
                merge2_odd(odd_list[at - begun - 1])
        for at in range(pairs + 1 - begun, pairs):
            merge2_odd(odd_list[at])
        for p in range(pairs):
            cross3[p].wait_send()
        when_do(has_below, halo3[0].wait_send)
        when_do(has_above, halo3[1].wait_send)

    for copies in (cross0, cross1):
        for copy in copies:
            copy.wait_send()
    for copies in (halo0, halo1):
        when_do(has_below, copies[0].wait_send)
        when_do(has_above, copies[1].wait_send)


def shards(view_blocks, shifts, taps, ztaps):
    _, planes, rows, width = view_blocks.shape
    pairs = planes // 2
    margin = width // 8 + LANES
    blocks = (width + 2 * margin) // LANES
    bf16 = jnp.bfloat16
    dma = pltpu.SemaphoreType.DMA
    vmem = pltpu.VMEM
    result = pl.pallas_call(
        functools.partial(kernel, pairs, width, margin, taps.shape[2]),
        out_shape=jax.ShapeDtypeStruct((pairs, 16, width), bf16),
        in_specs=[pl.BlockSpec(memory_space=pl.ANY)]
        + [pl.BlockSpec(memory_space=pltpu.SMEM)] * 3,
        out_specs=pl.BlockSpec(memory_space=pltpu.VMEM),
        scratch_shapes=[
            vmem((planes, rows, width), bf16),
            vmem((2, rows, width), bf16),
            vmem((blocks, 2 * rows, LANES), bf16),
            vmem((blocks, rows, LANES), bf16),
            vmem((blocks, rows // 2, LANES), bf16),
            vmem((3, WINDOW, BLOCK), bf16),
            vmem((pairs, rows, width), bf16),
            vmem((pairs, rows, width), bf16),
            vmem((pairs, rows, width), bf16),
            vmem((2, rows // 2, width), bf16),
            vmem((2, rows // 2, width), bf16),
            vmem((pairs, rows // 2, width), bf16),
            vmem((pairs, rows // 2, width), bf16),
            vmem((pairs, rows // 2, width), bf16),
            vmem((2, rows // 4, width), bf16),
            vmem((2, rows // 4, width), bf16),
            vmem((pairs, rows, width), bf16),
            vmem((2, rows // 2, width), bf16),
            vmem((2, rows // 2, width), bf16),
            vmem((pairs, rows // 4, width), bf16),
            vmem((pairs, rows // 4, width), bf16),
            vmem((pairs, rows // 4, width), bf16),
            dma((pairs,)),
            dma((pairs,)),
            dma((pairs,)),
            dma((pairs,)),
            dma((pairs,)),
            dma((pairs,)),
            dma((pairs,)),
            dma((4, 2)),
            dma((4, 2)),
        ],
        compiler_params=pltpu.CompilerParams(
            collective_id=0, has_side_effects=True, vmem_limit_bytes=58 * 1024 * 1024
        ),
        cost_estimate=pl.CostEstimate(
            flops=15_000_000_000, bytes_accessed=9 * 1024 * 1024, transcendentals=0
        ),
    )(view_blocks.reshape(planes, rows, width), shifts, taps, ztaps)
    return result.reshape(1, planes, 8, width)


def solution(mesh):
    return jax.shard_map(
        shards,
        mesh=mesh,
        in_specs=(P("views", "slab", None, None), P(), P(), P()),
        out_specs=P("views", "slab", None, None),
        check_vma=False,
    )
```

```python
import functools

import jax
import jax.numpy as jnp
from jax import lax
from jax.experimental import pallas as pl
from jax.experimental.pallas import tpu as pltpu
from jax.sharding import PartitionSpec as P

LANES = 128
BLOCK = 256
WINDOW = 512
STRIP = 512
MESH = pl.DeviceIdType.MESH


def kernel(
    pairs,
    width,
    margin,
    tap_count,
    x_hbm,
    shifts,
    taps,
    ztaps,
    out,
    xin,
    h0,
    mixed0,
    mixed1,
    mixed2,
    band,
    x1,
    s0,
    r0,
    h1s,
    h1r,
    x2,
    s1,
    r1,
    h2s,
    h2r,
    y1,
    h3s,
    h3r,
    k2,
    s2,
    r2,
    load_sem,
    s0_sem,
    r0_sem,
    s1_sem,
    r1_sem,
    s2_sem,
    r2_sem,
    hs_sem,
    hr_sem,
):
    view = lax.axis_index("views")
    slab = lax.axis_index("slab")
    last_slab = lax.axis_size("slab") - 1
    planes = 2 * pairs
    bit0 = view % 2
    bit1 = (view // 2) % 2
    bit2 = (view // 4) % 2
    core_peer = view + 1 - 2 * bit0
    near = view + 2 - 4 * bit1
    far = view + 4 - 8 * bit2
    peer1 = near + bit0 * (far - near)
    peer2 = far + bit0 * (near - far)
    first = bit1 + bit0 * (bit2 - bit1)
    second = bit2 + bit0 * (bit1 - bit2)
    even_core = bit0 == 0
    odd_core = bit0 == 1
    below = jnp.maximum(slab - 1, 0)
    above = jnp.minimum(slab + 1, last_slab)
    has_below = slab > 0
    has_above = slab < last_slab

    loads = [
        pltpu.make_async_copy(
            x_hbm.at[pl.ds(2 * p, 2)], xin.at[pl.ds(2 * p, 2)], load_sem.at[p]
        )
        for p in range(pairs)
    ]
    order0 = [(t + 1) % pairs for t in range(pairs)]
    for p in [0] + order0[:-1]:
        loads[p].start()

    barrier = pltpu.get_barrier_semaphore()
    for peer in (core_peer, peer1, peer2):
        pl.semaphore_signal(barrier, inc=1, device_id=(peer, slab), device_id_type=MESH)

    @pl.when(has_below)
    def _():
        pl.semaphore_signal(barrier, inc=1, device_id=(view, below), device_id_type=MESH)

    @pl.when(has_above)
    def _():
        pl.semaphore_signal(barrier, inc=1, device_id=(view, above), device_id_type=MESH)

    pl.semaphore_wait(
        barrier, 3 + has_below.astype(jnp.int32) + has_above.astype(jnp.int32)
    )

    def halo(level, src_down, src_up, landing):
        down = pltpu.make_async_remote_copy(
            src_down, landing.at[1], hs_sem.at[level, 0], hr_sem.at[level, 1],
            device_id=(view, below), device_id_type=MESH,
        )
        up = pltpu.make_async_remote_copy(
            src_up, landing.at[0], hs_sem.at[level, 1], hr_sem.at[level, 0],
            device_id=(view, above), device_id_type=MESH,
        )
        return down, up

    def when_do(condition, action):
        @pl.when(condition)
        def _():
            action()

    halo0 = halo(0, x_hbm.at[0], x_hbm.at[planes - 1], h0)
    halo1 = halo(1, h1s.at[0], h1s.at[1], h1r)
    halo2 = halo(2, h2s.at[0], h2s.at[1], h2r)
    halo3 = halo(3, h3s.at[0], h3s.at[1], h3r)
    when_do(has_below, halo0[0].start)
    when_do(has_above, halo0[1].start)

    def zero_ends(landing):
        @pl.when(jnp.logical_not(has_below))
        def _():
            landing[0] = jnp.zeros(landing.shape[1:], landing.dtype)

        @pl.when(jnp.logical_not(has_above))
        def _():
            landing[1] = jnp.zeros(landing.shape[1:], landing.dtype)

    for landing in (h0, h1r, h2r, h3r):
        zero_ends(landing)

    edge_blocks = margin // LANES
    mixes = [mixed0, mixed1, mixed2]
    for mixed in mixes:
        empty = jnp.zeros((edge_blocks,) + mixed.shape[1:], mixed.dtype)
        mixed[0:edge_blocks] = empty
        mixed[mixed.shape[0] - edge_blocks :] = empty

    groups = [view, view // 2, view // 4]
    bases = []
    scales = []
    candidates = 1.0 + (
        lax.broadcasted_iota(jnp.int32, (8, LANES), 0) * LANES
        + lax.broadcasted_iota(jnp.int32, (8, LANES), 1)
    ).astype(jnp.float32) * (1.0 / (8 * LANES))
    for level in range(3):
        start = shifts[level, groups[level]] + (margin - 1)
        base = lax.div(start, jnp.int32(LANES))
        offset = start - base * LANES
        bases.append(base)
        distance = (
            lax.broadcasted_iota(jnp.int32, (WINDOW, BLOCK), 0)
            - lax.broadcasted_iota(jnp.int32, (WINDOW, BLOCK), 1)
            - offset
        )
        worst = jnp.zeros((8, LANES), jnp.float32)
        for k in range(tap_count):
            tap = taps[level, groups[level] * tap_count + k]
            exact = tap * candidates
            missed = jnp.abs(exact.astype(jnp.bfloat16).astype(jnp.float32) - exact)
            worst = jnp.maximum(worst, missed / jnp.maximum(exact, 1e-30))
        chosen = jnp.where(worst == jnp.min(worst), candidates, 0.0)
        scale = jnp.max(chosen)
        scales.append(1.0 / scale)
        values = jnp.zeros((WINDOW, BLOCK), jnp.float32)
        for k in range(tap_count):
            values = jnp.where(distance == k, taps[level, groups[level] * tap_count + k] * scale, values)
        band[level] = (0.5 * values).astype(jnp.bfloat16)

    def weights(level):
        return [ztaps[level, groups[level] * 3 + i] * scales[level] for i in range(3)]

    def strips(body):
        def step(i, carry):
            body(pl.multiple_of(i * STRIP, STRIP))
            return carry

        lax.fori_loop(0, width // STRIP, step, 0, unroll=2)

    def f32(value):
        return value.astype(jnp.float32)

    def put(level, row, col, lower, upper):
        value = jnp.concatenate([lower, upper], 0).astype(jnp.bfloat16)
        at = lax.div(col, LANES) + edge_blocks
        for i in range(STRIP // LANES):
            mixes[level][at + i, pl.ds(row, 16), :] = value[:, i * LANES : (i + 1) * LANES]

    def mix_first(p):
        w = weights(0)

        def body(col):
            cols = pl.ds(col, STRIP)
            for part in range(2):
                side = bit0 if part == 0 else 1 - bit0
                for i in range(2):
                    rows = pl.ds(pl.multiple_of(32 * side + 16 * i, 16), 16)
                    a = f32(h0[0, rows, cols] if p == 0 else xin[2 * p - 1, rows, cols])
                    b = f32(xin[2 * p, rows, cols])
                    c = f32(xin[2 * p + 1, rows, cols])
                    d = f32(h0[1, rows, cols] if p == pairs - 1 else xin[2 * p + 2, rows, cols])
                    lower = w[0] * a + w[1] * b + w[2] * c
                    upper = w[0] * b + w[1] * c + w[2] * d
                    slots = (0, 1 + side) if i == 0 else (2 - side, 3)
                    for half in range(2):
                        row = pl.multiple_of(64 * part + 16 * slots[half], 16)
                        put(
                            0, row, col,
                            lower[8 * half : 8 * half + 8],
                            upper[8 * half : 8 * half + 8],
                        )

        strips(body)

    def mix_later(level, p, target, source, landing, chunk_starts):
        w = weights(level)

        def body(col):
            cols = pl.ds(col, STRIP)
            for at, chunk in enumerate(chunk_starts):
                even = at % 2 if len(chunk_starts) > 2 else None
                rows = pl.ds(pl.multiple_of(16 * chunk, 16), 16)
                here = f32(source[p, rows, cols])
                b, c = here[:8], here[8:]

                def edge(end):
                    if even is None:
                        block = f32(landing[end, 0:16, cols])
                        return jnp.where(chunk == 0, block[:8], block[8:])
                    block = f32(
                        landing[end, pl.ds(pl.multiple_of(8 * (chunk - even), 16), 16), cols]
                    )
                    return block[8 * even : 8 * even + 8]

                a = edge(0) if p == 0 else f32(source[p - 1, rows, cols])[8:]
                d = edge(1) if p == pairs - 1 else f32(source[p + 1, rows, cols])[:8]
                lower = w[0] * a + w[1] * b + w[2] * c
                upper = w[0] * b + w[1] * c + w[2] * d
                put(target, 16 * at, col, lower, upper)

        strips(body)

    def interpolate(level, p, target, kept, sent):
        mixed = mixes[target]
        rows = mixed.shape[1]
        together = max(1, 512 // rows)
        base = bases[level]
        half = rows // 2

        def step(group, carry):
            windows = []
            for j in range(together):
                at = base + (BLOCK // LANES) * (group * together + j)
                windows.append(
                    jnp.concatenate([mixed[at + i] for i in range(WINDOW // LANES)], 1)
                )
            operand = jnp.concatenate(windows, 0)
            total = jnp.dot(operand, band[level], preferred_element_type=jnp.float32)
            for j in range(together):
                cols = pl.ds(pl.multiple_of((group * together + j) * BLOCK, BLOCK), BLOCK)
                piece = total[j * rows : (j + 1) * rows].astype(jnp.bfloat16)
                kept[p, :, cols] = piece[:half]
                sent[p, :, cols] = piece[half:]
            return carry

        lax.fori_loop(0, width // (BLOCK * together), step, 0, unroll=2 if level < 2 else 1)

    def add_into(target, p, kept, received):
        def body(col):
            cols = pl.ds(col, STRIP)
            target[p, :, cols] = (f32(kept[p, :, cols]) + f32(received[p, :, cols])).astype(
                jnp.bfloat16
            )

        strips(body)

    def exchange(sent, received, send_sem, recv_sem, peer):
        return [
            pltpu.make_async_remote_copy(
                sent.at[p], received.at[p], send_sem.at[p], recv_sem.at[p],
                device_id=(peer, slab), device_id_type=MESH,
            )
            for p in range(pairs)
        ]

    cross0 = exchange(s0, r0, s0_sem, r0_sem, core_peer)
    cross1 = exchange(s1, r1, s1_sem, r1_sem, peer1)
    cross2 = exchange(s2, r2, s2_sem, r2_sem, peer2)
    sent_rows = pl.ds(pl.multiple_of(16 - 16 * second, 16), 16)
    kept_rows = pl.ds(pl.multiple_of(16 * second, 16), 16)
    cross3 = exchange(x2.at[:, sent_rows], r2, s2_sem, r2_sem, peer2)

    def send_edges(p, source, ready, copies, chunks):
        for end, at, half in ((0, 0, 0), (1, pairs - 1, 8)):
            if p != at:
                continue

            def body(col):
                cols = pl.ds(col, STRIP)
                for c in range(0, chunks, 2):
                    one = f32(source[p, 16 * c : 16 * c + 16, cols])[half : half + 8]
                    two = f32(source[p, 16 * c + 16 : 16 * c + 32, cols])[half : half + 8]
                    ready[end, 8 * c : 8 * c + 16, cols] = jnp.concatenate([one, two], 0).astype(
                        jnp.bfloat16
                    )

            strips(body)
            when_do(has_below if end == 0 else has_above, copies[end].start)

    loaded = set()

    def need(p):
        if 0 <= p < pairs and p not in loaded:
            loads[p].wait()
            loaded.add(p)

    def await_halo(p, copies):
        if p == 0:
            when_do(has_below, copies[1].wait_recv)
        if p == pairs - 1:
            when_do(has_above, copies[0].wait_recv)

    def level0(p):
        for q in (p - 1, p, p + 1):
            need(q)
        await_halo(p, halo0)
        mix_first(p)
        interpolate(0, p, 0, x1, s0)
        cross0[p].start()

    def merge0(p):
        cross0[p].wait_recv()
        add_into(x1, p, x1, r0)
        send_edges(p, x1, h1s, halo1, 4)

    own, other = 2 * first, 2 - 2 * first

    def level1_even(p):
        mix_later(1, p, 1, x1, h1r, [own, own + 1, other, other + 1])
        interpolate(1, p, 1, x2, s1)
        cross1[p].start()

    def merge1_even(p):
        cross1[p].wait_recv()
        add_into(x2, p, x2, r1)
        send_edges(p, x2, h2s, halo2, 2)

    def level2_even(p):
        await_halo(p, halo2)
        mix_later(2, p, 2, x2, h2r, [second, 1 - second])
        interpolate(2, p, 2, k2, s2)
        cross2[p].start()

    def merge2_even(p):
        cross2[p].wait_recv()
        add_into(out, p, k2, r2)

    def level1_odd(p):
        mix_later(1, p, 1, x1, h1r, [0, 1, 2, 3])
        interpolate(1, p, 1, y1.at[:, 0:32], y1.at[:, 32:64])
        send_edges(p, y1, h3s, halo3, 4)

    def level2_odd(p):
        await_halo(p, halo3)
        mix_later(2, p, 1, y1, h3r, [own, own + 1, other, other + 1])
        interpolate(2, p, 1, x2, s1)
        cross1[p].start()

    def merge1_odd(p):
        cross1[p].wait_recv()
        add_into(x2, p, x2, r1)
        cross3[p].start()

    def merge2_odd(p):
        cross3[p].wait_recv()
        add_into(out, p, x2.at[:, kept_rows], r2)

    final = pairs - 1
    late_inner = list(range(3, pairs - 2))
    odd_early = {5: late_inner[0], 7: late_inner[1]}

    def run(steps):
        for action, p in steps:
            action(p)

    def run_even(steps):
        @pl.when(even_core)
        def _():
            run(steps)

    def run_odd(steps):
        @pl.when(odd_core)
        def _():
            run(steps)

    for t in range(pairs + 1):
        if t < pairs:
            level0((t + 1) % pairs)
        if t >= 1:
            merge0(t % pairs)
        if t >= 3:
            p = t - 1 if t < pairs else 1
            run_even([(level1_even, p)])
            run_odd([(level1_odd, p)])
        if t in odd_early:
            run_odd([(level2_odd, odd_early[t])])

    arrivals = list(range(2, pairs - 1)) + [1, final, 0]
    run_even([(merge1_even, p) for p in arrivals[:3]] + [(level2_even, 3)])
    run_odd(
        [(level2_odd, p) for p in late_inner[2:] + [2]] + [(merge1_odd, late_inner[0])]
    )
    for p in (final, 0):
        await_halo(p, halo1)
        run_even([(level1_even, p)])
        run_odd([(level1_odd, p)])

    even_steps = []
    for p in arrivals[3:]:
        even_steps.append((merge1_even, p))
        if 5 <= p < final:
            even_steps.append((level2_even, p - 1))
        if p == 1:
            even_steps.append((level2_even, 2))
            even_steps.append((merge2_even, 3))
        if p == final:
            even_steps.append((level2_even, final - 1))
            even_steps.append((merge2_even, 4))
    even_steps.append((level2_even, 1))
    even_steps += [(merge2_even, p) for p in list(range(5, final - 1)) + [2]]
    even_steps += [(level2_even, final), (level2_even, 0)]
    even_steps += [(merge2_even, p) for p in (final - 1, 1, final, 0)]

    odd_inner = late_inner + [2]
    odd_steps = [(level2_odd, final - 1), (level2_odd, 1)]
    odd_steps += [(merge1_odd, p) for p in odd_inner[1:]]
    odd_steps += [(merge2_odd, p) for p in odd_inner[:2]]
    odd_steps += [(level2_odd, final), (level2_odd, 0)]
    odd_steps += [(merge1_odd, final - 1), (merge1_odd, 1)]
    odd_steps += [(merge2_odd, p) for p in odd_inner[2:]]
    odd_steps += [(merge1_odd, final), (merge1_odd, 0)]
    odd_steps += [(merge2_odd, p) for p in (final - 1, 1, final, 0)]

    @pl.when(even_core)
    def _():
        run(even_steps)
        for p in range(pairs):
            cross2[p].wait_send()
        when_do(has_below, halo2[0].wait_send)
        when_do(has_above, halo2[1].wait_send)

    @pl.when(odd_core)
    def _():
        run(odd_steps)
        for p in range(pairs):
            cross3[p].wait_send()
        when_do(has_below, halo3[0].wait_send)
        when_do(has_above, halo3[1].wait_send)

    for copies in (cross0, cross1):
        for copy in copies:
            copy.wait_send()
    for copies in (halo0, halo1):
        when_do(has_below, copies[0].wait_send)
        when_do(has_above, copies[1].wait_send)


def shards(view_blocks, shifts, taps, ztaps):
    _, planes, rows, width = view_blocks.shape
    pairs = planes // 2
    margin = width // 8 + LANES
    blocks = (width + 2 * margin) // LANES
    bf16 = jnp.bfloat16
    dma = pltpu.SemaphoreType.DMA
    vmem = pltpu.VMEM
    result = pl.pallas_call(
        functools.partial(kernel, pairs, width, margin, taps.shape[2]),
        out_shape=jax.ShapeDtypeStruct((pairs, 16, width), bf16),
        in_specs=[pl.BlockSpec(memory_space=pl.ANY)]
        + [pl.BlockSpec(memory_space=pltpu.SMEM)] * 3,
        out_specs=pl.BlockSpec(memory_space=pltpu.VMEM),
        scratch_shapes=[
            vmem((planes, rows, width), bf16),
            vmem((2, rows, width), bf16),
            vmem((blocks, 2 * rows, LANES), bf16),
            vmem((blocks, rows, LANES), bf16),
            vmem((blocks, rows // 2, LANES), bf16),
            vmem((3, WINDOW, BLOCK), bf16),
            vmem((pairs, rows, width), bf16),
            vmem((pairs, rows, width), bf16),
            vmem((pairs, rows, width), bf16),
            vmem((2, rows // 2, width), bf16),
            vmem((2, rows // 2, width), bf16),
            vmem((pairs, rows // 2, width), bf16),
            vmem((pairs, rows // 2, width), bf16),
            vmem((pairs, rows // 2, width), bf16),
            vmem((2, rows // 4, width), bf16),
            vmem((2, rows // 4, width), bf16),
            vmem((pairs, rows, width), bf16),
            vmem((2, rows // 2, width), bf16),
            vmem((2, rows // 2, width), bf16),
            vmem((pairs, rows // 4, width), bf16),
            vmem((pairs, rows // 4, width), bf16),
            vmem((pairs, rows // 4, width), bf16),
            dma((pairs,)),
            dma((pairs,)),
            dma((pairs,)),
            dma((pairs,)),
            dma((pairs,)),
            dma((pairs,)),
            dma((pairs,)),
            dma((4, 2)),
            dma((4, 2)),
        ],
        compiler_params=pltpu.CompilerParams(
            collective_id=0, has_side_effects=True, vmem_limit_bytes=58 * 1024 * 1024
        ),
        cost_estimate=pl.CostEstimate(
            flops=15_000_000_000, bytes_accessed=9 * 1024 * 1024, transcendentals=0
        ),
    )(view_blocks.reshape(planes, rows, width), shifts, taps.reshape(taps.shape[0], -1), ztaps.reshape(ztaps.shape[0], -1))
    return result.reshape(1, planes, 8, width)


def solution(mesh):
    return jax.shard_map(
        shards,
        mesh=mesh,
        in_specs=(P("views", "slab", None, None), P(), P(), P()),
        out_specs=P("views", "slab", None, None),
        check_vma=False,
    )
```
